32 devices in a mesh: member: 4 (over z), lat: 4 (over y, core), lon: 2 (over x).
Axes of the slice: x: 2, y: 2, z: 4, core: 2. Of those that a mesh axis runs over, the one named last changes fastest.
Arguments:
- fields: float32 [8, 32, 160, 1024], P('member', None, 'lat', 'lon'), may hold values from -6 to 6
- spectra: float32 [9, 513], replicated, may hold values from 0.3 to 1.5
- band_weights: float32 [9, 160, 5], P(None, 'lat'), may hold values from -2.5 to 2.5
- band_start: int32 [160], P('lat'), may hold values from 0 to 155, as said below
- depth_weights: float32 [32, 9], replicated, may hold values from -2 to 2
- mix_weights: float32 [32, 32], replicated, may hold values from -1 to 1
- target: float32 [32, 160, 1024], P('member', 'lat', 'lon'), may hold values from -6 to 6
Outputs:
- crps: float32 [32, 160, 1024], P('member', 'lat', 'lon')
The draws below stay inside these ranges and needn't reach their ends.
Inputs may be any that keep to these rules, and one draw needn't show every extreme that they name: For each output row o, band_start[o] lies between o - 5 and o + 5 - 5 + 1; both ends of that offset range occur.
All inputs are finite; a program needn't handle non-finite values.
Results may differ from the reference program's by a relative error of at most 0.0001.
Values sent between devices are 32-bit elements; how exact they have to be, the bound alone decides.
A program may use at most 128 MiB of HBM per device.

```python
import math
import jax
import jax.numpy as jnp
from jax import lax

C = 32
NLON = 1024
KB = 9
BAND = 5
REACH = 5
M = 8
NLAT = 160
NF = 513


def draw_band_start(key, part):
    row_idx = jnp.arange(NLAT, dtype=jnp.int32)
    jitter = jax.random.randint(key, (NLAT,), 0, 2 * REACH - BAND + 2, dtype=jnp.int32)
    jitter = jnp.where(row_idx % 7 == 0, 0, jitter)
    jitter = jnp.where(row_idx % 7 == 3, 2 * REACH - BAND + 1, jitter)
    start_row = jnp.clip(row_idx - REACH + jitter, 0, NLAT - BAND)
    start_row = jnp.where(row_idx == NLAT - 1, NLAT - BAND, start_row)
    return start_row.astype(jnp.int32)


def block_scale(stream_key, dims, cuts, low, largest):
    loudness, own = 1.0, jax.random.fold_in(stream_key, 6)
    for axis_at, parts in cuts:
        steps = jnp.exp(jax.random.uniform(jax.random.fold_in(own, axis_at), (parts,), jnp.float32, low / len(cuts), largest / len(cuts)))
        loudness = loudness * jnp.repeat(steps, dims[axis_at] // parts).reshape([-1 if axis == axis_at else 1 for axis in range(len(dims))])
    return loudness


def normal_values(own_key, shape, scale, limit, shards=(), held_as=jnp.bfloat16):
    values = jax.random.normal(own_key, shape, jnp.float32) * scale
    if len(shards) > 0:
        values = block_scale(own_key, shape, shards, -0.22, 0.18) * values
    return jnp.clip(values, min=-limit, max=limit).astype(held_as)


def setup_inputs(seed: int = 0) -> dict:
    splits = jax.random.split(jax.random.key(seed), 8)
    return {
        "fields": normal_values(splits[0], (M, C, NLAT, NLON), 1.0, 6.0, ((0, 4), (2, 4), (3, 2)), jnp.float32),
        "spectra": jnp.clip(jnp.exp(jax.random.uniform(splits[1], (KB, NF), jnp.float32, math.log(0.3), math.log(1.5))), 0.3, 1.5),
        "band_weights": normal_values(splits[2], (KB, NLAT, BAND), BAND ** -0.5, 2.5, ((1, 4),), jnp.float32),
        "band_start": draw_band_start(jax.random.fold_in(splits[7], 71), 0),
        "depth_weights": normal_values(splits[4], (C, KB), KB ** -0.5, 2.0, (), jnp.float32),
        "mix_weights": normal_values(splits[5], (C, C), C ** -0.5, 1.0, (), jnp.float32),
        "target": normal_values(splits[6], (C, NLAT, NLON), 1.0, 6.0, ((0, 4), (1, 4), (2, 2)), jnp.float32),
    }


def pair_total(ensemble):
    def step(member_idx, acc_sum):
        picked = lax.dynamic_index_in_dim(ensemble, member_idx, 0, keepdims=True)
        return acc_sum + jnp.sum(jnp.abs(picked - ensemble), axis=0)

    start_sum = jnp.zeros(ensemble.shape[1:], jnp.float32)
    return lax.fori_loop(0, ensemble.shape[0], step, start_sum)


def reference(fields, spectra, band_weights, band_start, depth_weights, mix_weights, target):
    offsets = jnp.arange(BAND, dtype=jnp.int32)
    read_rows = band_start.astype(jnp.int32)[:, None] + offsets[None, :]

    def one_member(field):
        spectrum = jnp.fft.rfft(field, axis=-1)
        summed = jnp.zeros_like(spectrum)
        for basis_idx in range(KB):
            band_sum = jnp.zeros_like(spectrum)
            for offset_idx in range(BAND):
                band_sum = band_sum + band_weights[basis_idx, :, offset_idx][None, :, None] * spectrum[:, read_rows[:, offset_idx], :]
            summed = summed + depth_weights[:, basis_idx][:, None, None] * spectra[basis_idx][None, None, :] * band_sum
        smooth = jnp.fft.irfft(summed, n=NLON, axis=-1)
        mixed_out = jnp.einsum("dc,cal->dal", mix_weights, smooth, precision=lax.Precision.HIGHEST)
        return jax.nn.gelu(mixed_out, approximate=False)

    hidden = lax.map(one_member, fields)
    members = hidden.shape[0]
    skill_term = jnp.mean(jnp.abs(hidden - target[None]), axis=0)
    spread = pair_total(hidden)
    return skill_term - spread / (2.0 * members * members)
```

```python
import functools
import math

import jax
import jax.numpy as jnp
import numpy as np
from jax import lax
from jax.experimental import pallas as pl
from jax.experimental.pallas import tpu as pltpu
from jax.sharding import PartitionSpec as P

REACH = 5
CHUNK = 8
HIGH = lax.Precision.HIGH


def tables(length):
    half = length // 2
    column = np.arange(length)
    is_cosine = column <= half
    frequency = np.where(is_cosine, column, column - half)
    angle = (np.arange(length)[:, None] * frequency[None, :] % length) * (2.0 * math.pi / length)
    forward = np.where(is_cosine[None, :], np.cos(angle), np.sin(angle))
    edge = is_cosine & ((frequency == 0) | (frequency == half))
    inverse = (forward * np.where(edge, 1.0, 2.0)[None, :] / length).T
    return forward.astype(np.float32), inverse.astype(np.float32)


def shifted(value, axis, shift):
    size = lax.axis_size(axis)
    return lax.ppermute(value, axis, [(i, (i + shift) % size) for i in range(size)])


def band_kernel(n_basis, band_len, starts_ref, weights_ref, factor_ref, *refs):
    rows, out_ref = refs[:band_len], refs[band_len]
    row = pl.program_id(0)
    members, length = out_ref.shape[1], out_ref.shape[3]
    scalars = [
        [weights_ref[(row * n_basis + k) * band_len + j] for j in range(band_len)]
        for k in range(n_basis)
    ]
    width = 128
    for tile in range(length // width):
        lanes = pl.ds(tile * width, width)
        gains = [None] * band_len
        for k in range(n_basis):
            factor = factor_ref[k, :, lanes]
            for j in range(band_len):
                term = scalars[k][j] * factor
                gains[j] = term if k == 0 else gains[j] + term
        for m in range(members):
            total = gains[0] * rows[0][0, m, :, lanes]
            for j in range(1, band_len):
                total = total + gains[j] * rows[j][0, m, :, lanes]
            out_ref[0, m, :, lanes] = total


def band_rows(source, starts, weights, factor):
    n_basis, n_rows, band_len = weights.shape
    _, members, own, length = source.shape
    flat = weights.transpose(1, 0, 2).reshape(-1)

    def pick(j):
        return pl.BlockSpec((1, members, own, length), lambda o, s: (s[o] + j, 0, 0, 0))

    return pl.pallas_call(
        functools.partial(band_kernel, n_basis, band_len),
        grid_spec=pltpu.PrefetchScalarGridSpec(
            num_scalar_prefetch=1,
            grid=(n_rows,),
            in_specs=[
                pl.BlockSpec(memory_space=pltpu.SMEM),
                pl.BlockSpec(factor.shape, lambda o, s: (0, 0, 0)),
            ]
            + [pick(j) for j in range(band_len)],
            out_specs=pl.BlockSpec((1, members, own, length), lambda o, s: (o, 0, 0, 0)),
        ),
        out_shape=jax.ShapeDtypeStruct((n_rows, members, own, length), jnp.float32),
        compiler_params=pltpu.CompilerParams(vmem_limit_bytes=16 * 1024 * 1024),
        cost_estimate=pl.CostEstimate(
            flops=2 * n_rows * own * length * band_len * (n_basis + members) * 16,
            bytes_accessed=4 * n_rows * (band_len + 1) * members * own * length,
            transcendentals=0,
        ),
    )(starts, flat, factor, *([source] * band_len))


def score(pieces, analysis):
    ensemble = [p[:, m] for p in pieces for m in range(p.shape[1])]
    count = len(ensemble)
    skill = sum(jnp.abs(h - analysis) for h in ensemble) / count
    spread = sum(
        jnp.abs(ensemble[i] - ensemble[j]) for i in range(count) for j in range(i + 1, count)
    )
    return skill - spread / (count * count)


def local(fields, spectra, band_weights, band_start, depth_weights, mix_weights, target):
    members, variables, n_rows, seg = fields.shape
    n_lon, n_member = lax.axis_size("lon"), lax.axis_size("member")
    lon, me = lax.axis_index("lon"), lax.axis_index("member")
    own, group = variables // n_lon, variables // n_member
    length = seg * n_lon
    forward, inverse = tables(length)
    forward = jnp.asarray(forward.reshape(n_lon, seg, length))
    inverse = jnp.asarray(np.ascontiguousarray(inverse.reshape(length, n_lon, seg).transpose(1, 0, 2)))

    def at(value, index, axis=0):
        return lax.dynamic_index_in_dim(value, index, axis, keepdims=False)

    by_owner = fields.reshape(members, n_lon, own, n_rows, seg)
    spectrum = None
    for s in range(n_lon):
        piece = at(by_owner, (lon + s) % n_lon, 1).transpose(2, 0, 1, 3)
        if s > 0:
            piece = shifted(piece, "lon", s)
        part = jnp.dot(
            piece.reshape(-1, seg),
            at(forward, (lon + n_lon - s) % n_lon),
            precision=HIGH,
            preferred_element_type=jnp.float32,
        )
        spectrum = part if spectrum is None else spectrum + part
    spectrum = spectrum.reshape(n_rows, members, own, length)

    size = lax.axis_size("lat")
    up = [(i, i + 1) for i in range(size - 1)]
    before = lax.ppermute(spectrum[n_rows - REACH :], "lat", up)
    after = lax.ppermute(spectrum[:REACH], "lat", [(j, i) for i, j in up])

    half_spec = jnp.concatenate([spectra, spectra[:, 1:-1]], axis=1)
    depth_own = lax.dynamic_slice_in_dim(depth_weights, lon * own, own, 0)
    factor = depth_own.T[:, :, None] * half_spec[:, None, :]
    starts = band_start - lax.axis_index("lat") * n_rows

    chunk = CHUNK if n_rows % CHUNK == 0 else n_rows
    rm = chunk * members
    mix_rolled = jnp.stack(
        [at(mix_weights.reshape(n_member, group, variables), (me + s) % n_member) for s in range(n_member)]
    ).reshape(n_member, group, n_lon, own)
    eye = jnp.eye(rm, dtype=jnp.float32)
    mixers = []
    for s in range(n_lon):
        block = at(mix_rolled, (lon + n_lon - s) % n_lon, 2)
        wide = block[:, None, :, None, :] * eye[None, :, None, :, None]
        mixers.append(wide.reshape(n_member * rm * group, rm * own))
    inverse_seg = [at(inverse, (lon + s) % n_lon) for s in range(n_lon)]

    chunks = n_rows // chunk
    inner = [q for q in range(chunks) if q * chunk >= REACH and (q + 1) * chunk + REACH <= n_rows]
    order = inner + [q for q in range(chunks) if q not in inner]
    results = [None] * chunks
    for q in order:
        low, high = q * chunk, (q + 1) * chunk
        first = 0
        source = spectrum
        if q not in inner:
            first, last = max(low - REACH, 0), min(high + REACH, n_rows)
            parts = [spectrum[first:last]]
            if low < REACH:
                parts, first = [before] + parts, -REACH
            if high + REACH > n_rows:
                parts = parts + [after]
            source = jnp.concatenate(parts, axis=0)
        filtered = band_rows(source, starts[low:high] - first, band_weights[:, low:high], factor)
        filtered = filtered.reshape(rm * own, length)
        mixed = None
        for s in range(n_lon):
            smooth = jnp.dot(
                filtered, inverse_seg[s], precision=HIGH, preferred_element_type=jnp.float32
            )
            if s > 0:
                smooth = shifted(smooth, "lon", s)
            part = jnp.dot(mixers[s], smooth, precision=HIGH, preferred_element_type=jnp.float32)
            mixed = part if mixed is None else mixed + part
        hidden = jax.nn.gelu(mixed, approximate=False)
        hidden = hidden.reshape(n_member, chunk, members, group, seg)
        pieces = [hidden[0]] + [shifted(hidden[s], "member", s) for s in range(1, n_member)]
        analysis = target[:, low:high].transpose(1, 0, 2)
        results[q] = score(pieces, analysis).transpose(1, 0, 2)
    return jnp.concatenate(results, axis=1)


def solution(mesh):
    in_specs = (
        P("member", None, "lat", "lon"),
        P(),
        P(None, "lat", None),
        P("lat"),
        P(),
        P(),
        P("member", "lat", "lon"),
    )
    out_specs = P("member", "lat", "lon")
    return jax.shard_map(local, mesh=mesh, in_specs=in_specs, out_specs=out_specs, check_vma=False)
```

```python
import functools
import math

import jax
import jax.numpy as jnp
import numpy as np
from jax import lax
from jax.experimental import pallas as pl
from jax.experimental.pallas import tpu as pltpu
from jax.sharding import PartitionSpec as P

REACH = 5
CHUNK = 8
HIGH = lax.Precision.HIGH


def tables(length):
    half = length // 2
    column = np.arange(length)
    is_cosine = column <= half
    frequency = np.where(is_cosine, column, column - half)
    angle = (np.arange(length)[:, None] * frequency[None, :] % length) * (2.0 * math.pi / length)
    forward = np.where(is_cosine[None, :], np.cos(angle), np.sin(angle))
    edge = is_cosine & ((frequency == 0) | (frequency == half))
    inverse = (forward * np.where(edge, 1.0, 2.0)[None, :] / length).T
    return forward.astype(np.float32), inverse.astype(np.float32)


def shifted(value, axis, shift):
    size = lax.axis_size(axis)
    return lax.ppermute(value, axis, [(i, (i + shift) % size) for i in range(size)])


def band_kernel(n_basis, band_len, starts_ref, weights_ref, factor_ref, *refs):
    rows, out_ref = refs[:band_len], refs[band_len]
    row = pl.program_id(0)
    members, length = out_ref.shape[1], out_ref.shape[3]
    scalars = [
        [weights_ref[(row * n_basis + k) * band_len + j] for j in range(band_len)]
        for k in range(n_basis)
    ]
    width = 128
    for tile in range(length // width):
        lanes = pl.ds(tile * width, width)
        gains = [None] * band_len
        for k in range(n_basis):
            factor = factor_ref[k, :, lanes]
            for j in range(band_len):
                term = scalars[k][j] * factor
                gains[j] = term if k == 0 else gains[j] + term
        for m in range(members):
            total = gains[0] * rows[0][0, m, :, lanes]
            for j in range(1, band_len):
                total = total + gains[j] * rows[j][0, m, :, lanes]
            out_ref[0, m, :, lanes] = total


def band_rows(source, starts, weights, factor):
    n_basis, n_rows, band_len = weights.shape
    _, members, own, length = source.shape
    flat = weights.transpose(1, 0, 2).reshape(-1)

    def pick(j):
        return pl.BlockSpec((1, members, own, length), lambda o, s: (s[o] + j, 0, 0, 0))

    return pl.pallas_call(
        functools.partial(band_kernel, n_basis, band_len),
        grid_spec=pltpu.PrefetchScalarGridSpec(
            num_scalar_prefetch=1,
            grid=(n_rows,),
            in_specs=[
                pl.BlockSpec(memory_space=pltpu.SMEM),
                pl.BlockSpec(factor.shape, lambda o, s: (0, 0, 0)),
            ]
            + [pick(j) for j in range(band_len)],
            out_specs=pl.BlockSpec((1, members, own, length), lambda o, s: (o, 0, 0, 0)),
        ),
        out_shape=jax.ShapeDtypeStruct((n_rows, members, own, length), jnp.float32),
        compiler_params=pltpu.CompilerParams(vmem_limit_bytes=16 * 1024 * 1024),
        cost_estimate=pl.CostEstimate(
            flops=2 * n_rows * own * length * band_len * (n_basis + members) * 16,
            bytes_accessed=4 * n_rows * (band_len + 1) * members * own * length,
            transcendentals=0,
        ),
    )(starts, flat, factor, *([source] * band_len))


def score(pieces, analysis):
    ensemble = [p[:, m] for p in pieces for m in range(p.shape[1])]
    count = len(ensemble)
    skill = sum(jnp.abs(h - analysis) for h in ensemble) / count
    spread = sum(
        jnp.abs(ensemble[i] - ensemble[j]) for i in range(count) for j in range(i + 1, count)
    )
    return skill - spread / (count * count)


def local(fields, spectra, band_weights, band_start, depth_weights, mix_weights, target):
    members, variables, n_rows, seg = fields.shape
    n_lon, n_member = lax.axis_size("lon"), lax.axis_size("member")
    lon = lax.axis_index("lon")
    own, group = variables // n_lon, variables // n_member
    length = seg * n_lon
    forward, inverse = tables(length)
    forward = jnp.asarray(forward.reshape(n_lon, seg, length))
    inverse = jnp.asarray(np.ascontiguousarray(inverse.reshape(length, n_lon, seg).transpose(1, 0, 2)))

    def at(value, index, axis=0):
        return lax.dynamic_index_in_dim(value, index, axis, keepdims=False)

    by_owner = fields.reshape(members, n_lon, own, n_rows, seg)
    chunk = CHUNK if n_rows % CHUNK == 0 else n_rows
    cut = 3 * chunk if n_rows > 3 * chunk else n_rows
    bands = [(0, cut)] + ([(cut, n_rows)] if cut < n_rows else [])
    spectra_of = []
    for low, high in bands:
        total = None
        for s in range(n_lon):
            piece = at(by_owner, (lon + s) % n_lon, 1)[:, :, low:high].transpose(2, 0, 1, 3)
            if s > 0:
                piece = shifted(piece, "lon", s)
            part = jnp.dot(
                piece.reshape(-1, seg),
                at(forward, (lon + n_lon - s) % n_lon),
                precision=HIGH,
                preferred_element_type=jnp.float32,
            )
            total = part if total is None else total + part
        spectra_of.append(total.reshape(high - low, members, own, length))

    size = lax.axis_size("lat")
    up = [(i, i + 1) for i in range(size - 1)]
    before = lax.ppermute(spectra_of[-1][-REACH:], "lat", up)
    after = lax.ppermute(spectra_of[0][:REACH], "lat", [(j, i) for i, j in up])
    pieces_of = (
        [(-REACH, 0, before)]
        + [(low, high, value) for (low, high), value in zip(bands, spectra_of)]
        + [(n_rows, n_rows + REACH, after)]
    )

    def source_rows(low, high):
        parts = []
        for first, last, value in pieces_of:
            if first <= low and high <= last:
                return value, first
            left, right = max(first, low), min(last, high)
            if left < right:
                parts.append(value[left - first : right - first])
        return jnp.concatenate(parts, axis=0), low

    half_spec = jnp.concatenate([spectra, spectra[:, 1:-1]], axis=1)
    depth_own = lax.dynamic_slice_in_dim(depth_weights, lon * own, own, 0)
    factor = depth_own.T[:, :, None] * half_spec[:, None, :]
    starts = band_start - lax.axis_index("lat") * n_rows

    rm = chunk * members
    mix_split = mix_weights.reshape(n_member, group, n_lon, own)
    eye = jnp.eye(rm, dtype=jnp.float32)
    mixers = []
    for s in range(n_lon):
        block = at(mix_split, (lon + n_lon - s) % n_lon, 2)
        wide = block[:, None, :, None, :] * eye[None, :, None, :, None]
        mixers.append(wide.reshape(n_member * rm * group, rm * own))
    inverse_seg = [at(inverse, (lon + s) % n_lon) for s in range(n_lon)]

    chunks = n_rows // chunk
    results = [None] * chunks
    for q in list(range(1, chunks)) + [0]:
        low, high = q * chunk, (q + 1) * chunk
        source, first = source_rows(low - REACH, high + REACH)
        filtered = band_rows(source, starts[low:high] - first, band_weights[:, low:high], factor)
        filtered = filtered.reshape(rm * own, length)
        mixed = None
        for s in range(n_lon):
            smooth = jnp.dot(
                filtered, inverse_seg[s], precision=HIGH, preferred_element_type=jnp.float32
            )
            if s > 0:
                smooth = shifted(smooth, "lon", s)
            part = jnp.dot(mixers[s], smooth, precision=HIGH, preferred_element_type=jnp.float32)
            mixed = part if mixed is None else mixed + part
        hidden = jax.nn.gelu(mixed, approximate=False)
        hidden = hidden.reshape(n_member, chunk, members, group, seg)
        gathered = lax.all_to_all(hidden, "member", split_axis=0, concat_axis=0)
        pieces = [gathered[s] for s in range(n_member)]
        analysis = target[:, low:high].transpose(1, 0, 2)
        results[q] = score(pieces, analysis).transpose(1, 0, 2)
    return jnp.concatenate(results, axis=1)


def solution(mesh):
    in_specs = (
        P("member", None, "lat", "lon"),
        P(),
        P(None, "lat", None),
        P("lat"),
        P(),
        P(),
        P("member", "lat", "lon"),
    )
    out_specs = P("member", "lat", "lon")
    return jax.shard_map(local, mesh=mesh, in_specs=in_specs, out_specs=out_specs, check_vma=False)
```
